128 devices in a mesh: samp: 64 (over x, y_hi, z, core), snp: 2 (over y_lo).
Axes of the slice: x: 4, y: 4 (y_hi: 2, y_lo: 2; y = y_hi * 2 + y_lo), z: 4, core: 2. Of those that a mesh axis runs over, the one named last changes fastest.
Arguments:
- dosage: bfloat16 [131072, 1024], P('samp', 'snp'), may hold values from -6 to 6
- pair_row: int32 [64, 4, 4096], P('samp'), may hold values from 0 to 2047
- pair_col: int32 [64, 4, 4096], P('samp'), may hold values from 0 to 2047
- pair_count: int32 [64, 4], P('samp'), may hold values from 512 to 4096, as said below
Outputs:
- sparse_grm: float32 [64, 4, 4096], P('samp', None, 'snp')
The draws below stay inside these ranges and needn't reach their ends.
Inputs may be any that keep to these rules, and one draw needn't show every extreme that they name: pair_count[b, s] is the number of leading live slots of block b at distance s; the largest, 4096, occurs in every draw.
All inputs are finite; a program needn't handle non-finite values.
Results may differ from the reference program's by a relative error of at most 0.0003.
Values may be sent and summed in bfloat16 or wider, within the bound.
A program may use at most 128 MiB of HBM per device.

```python
import jax
import jax.numpy as jnp
from jax import lax

BLK = 2048
SNPS = 1024
STOPS = 4
PAIRS = 4096
NBLK = 64
SAMPLES = 131072


def draw_pair_count(key, part):
    key = jax.random.fold_in(key, 5)
    first_key = jax.random.fold_in(key, 1)
    second_key = jax.random.fold_in(key, 2)
    lowest = max(1, PAIRS // 8)
    counts = jax.random.randint(first_key, (NBLK * STOPS,), lowest, PAIRS + 1, dtype=jnp.int32)
    position = jax.random.randint(second_key, (), 0, NBLK * STOPS, dtype=jnp.int32)
    counts = counts.at[position].set(PAIRS)
    return counts.reshape(NBLK, STOPS)


def touch_ends(drawn, stream_key, smallest, high):
    place = [jax.random.randint(jax.random.fold_in(stream_key, axis), (), 0, length) for axis, length in enumerate(drawn.shape)]
    widest = drawn.shape.index(max(drawn.shape))
    next_to = place[:widest] + [(place[widest] + 1) % drawn.shape[widest]] + place[widest + 1:]
    return drawn.at[tuple(place)].set(smallest).at[tuple(next_to)].set(high)


def shard_levels(rng, extent, split, least, top_value):
    factor_of = 1.0
    for dim, shards_of in split:
        steps = jax.random.uniform(jax.random.fold_in(jax.random.fold_in(rng, 6), dim), (shards_of,), jnp.float32, least / len(split), top_value / len(split))
        factor_of = factor_of * jnp.repeat(jnp.exp(steps), extent[dim] // shards_of).reshape((-1,) + (1,) * (len(extent) - 1 - dim))
    return factor_of


def normal_values(key, shape, scale, limit, split=(), held_as=jnp.bfloat16):
    array = scale * jax.random.normal(key, shape, jnp.float32)
    if split:
        array = array * shard_levels(key, shape, split, -0.22, 0.18)
    return jnp.clip(array, -limit, limit).astype(held_as)


def setup_inputs(seed: int = 0) -> dict:
    arg_keys = jax.random.split(jax.random.key(seed), 5)
    dosage = normal_values(arg_keys[0], (SAMPLES, SNPS), 1.0, 6.0, ((0, 64), (1, 2)))
    pair_row = touch_ends(jax.random.randint(arg_keys[1], (NBLK, STOPS, PAIRS), 0, BLK), jax.random.fold_in(arg_keys[1], 1), 0, BLK - 1).astype(jnp.int32)
    pair_col = touch_ends(jax.random.randint(arg_keys[2], (NBLK, STOPS, PAIRS), 0, BLK), jax.random.fold_in(arg_keys[2], 1), 0, BLK - 1).astype(jnp.int32)
    pair_count = draw_pair_count(jax.random.fold_in(arg_keys[4], 71), 0)
    return {"dosage": dosage, "pair_row": pair_row, "pair_col": pair_col, "pair_count": pair_count}


def reference(dosage, pair_row, pair_col, pair_count):
    blocks = dosage.reshape(NBLK, BLK, SNPS)

    def block_row(block_index):
        own_block = blocks[block_index]
        results = []
        for stop_index in range(STOPS):
            peer_index = ((block_index - stop_index) % NBLK).astype(jnp.int32)
            peer_block = blocks[peer_index]
            left_rows = own_block[pair_row[block_index, stop_index]].astype(jnp.float32)
            right_rows = peer_block[pair_col[block_index, stop_index]].astype(jnp.float32)
            products = jnp.sum(left_rows * right_rows, axis=1) / SNPS
            live_mask = jnp.arange(PAIRS, dtype=jnp.int32) < pair_count[block_index, stop_index]
            results.append(jnp.where(live_mask, products, jnp.zeros_like(products)))
        return jnp.stack(results)

    return lax.map(block_row, jnp.arange(NBLK, dtype=jnp.int32))
```

```python
import jax
import jax.numpy as jnp
from jax import lax
from jax.experimental import pallas as pl
from jax.experimental.pallas import tpu as pltpu
from jax.sharding import PartitionSpec as P

MESH = pl.DeviceIdType.MESH

BLK = 2048
HALF = 512
SNPS = 1024
STOPS = 4
PAIRS = 4096
NBLK = 64
CHUNKS = 8
CHUNK = BLK // CHUNKS
LIST = PAIRS // 128
SHARE = LIST // 2

OWN, ODD, EVEN, THIRD = 0, 1, 2, 3


def kernel(x, row_hbm, col_hbm, out, buf, tile0, tile1, row_v, col_v, addr_v, lane_v, addr_s, sums, land,
           own_sem, list_sem, addr_sem,
           odd_send, odd_recv, even_send, even_recv, third_send, third_recv, pass_send,
           ask_send, ask_recv, part_send, part_recv):
    samp = lax.axis_index("samp")
    snp = lax.axis_index("snp")
    core = lax.rem(samp, 2)
    chip = samp // 2
    even_core = core == 0
    odd_core = core == 1

    def device(chip_step, to_core, to_snp):
        to_chip = lax.rem(chip + (chip_step + NBLK // 2), NBLK // 2)
        return {"samp": to_chip * 2 + to_core, "snp": to_snp}

    sibling = device(0, 1 - core, snp)
    partner = device(0, core, 1 - snp)

    barrier = pltpu.get_barrier_semaphore()
    greeted = [sibling, partner]
    for chip_step in (-1, 1):
        for to_core in (0, 1):
            for to_snp in (snp, 1 - snp):
                greeted.append(device(chip_step, to_core, to_snp))
    for other in greeted:
        pl.semaphore_signal(barrier, inc=1, device_id=other, device_id_type=MESH)
    pl.semaphore_wait(barrier, len(greeted))

    def rows_of(n):
        return pl.ds(pl.multiple_of(n * CHUNK, CHUNK), CHUNK)

    def send_odd(n):
        return pltpu.make_async_remote_copy(
            x.at[rows_of(n)], buf.at[ODD, rows_of(n)], odd_send.at[n], odd_recv.at[n],
            device_id=device(1, 0, snp), device_id_type=MESH)

    def send_even(n):
        return pltpu.make_async_remote_copy(
            x.at[rows_of(n)], buf.at[EVEN, rows_of(n)], even_send.at[n], even_recv.at[n],
            device_id=device(1, 1, snp), device_id_type=MESH)

    def pass_odd(n):
        return pltpu.make_async_remote_copy(
            buf.at[ODD, rows_of(n)], buf.at[ODD, rows_of(n)], pass_send.at[n], odd_recv.at[n],
            device_id=sibling, device_id_type=MESH)

    def pass_even(n):
        return pltpu.make_async_remote_copy(
            buf.at[EVEN, rows_of(n)], buf.at[EVEN, rows_of(n)], pass_send.at[n], even_recv.at[n],
            device_id=sibling, device_id_type=MESH)

    def send_third(k):
        return pltpu.make_async_remote_copy(
            x, buf.at[THIRD], third_send.at[k], third_recv,
            device_id=device(-1, 0, snp) if k == 0 else sibling, device_id_type=MESH)

    @pl.when(odd_core)
    def _():
        for n in range(CHUNKS):
            send_odd(n).start()

    @pl.when(even_core)
    def _():
        send_third(0).start()
        send_third(1).start()

    load_own = pltpu.make_async_copy(x, buf.at[OWN], own_sem)
    load_own.start()
    load_row = pltpu.make_async_copy(row_hbm.at[0], row_v, list_sem.at[0])
    load_col = pltpu.make_async_copy(col_hbm.at[0], col_v, list_sem.at[1])
    load_row.start()
    load_col.start()
    load_row.wait()
    load_col.wait()

    distance = lax.broadcasted_iota(jnp.int32, (STOPS, 128), 0)
    swap = (distance == 3) & jnp.broadcast_to(even_core, (STOPS, 128))
    for k in range(LIST):
        rows = row_v[:, k * 128:(k + 1) * 128]
        cols = col_v[:, k * 128:(k + 1) * 128]
        down = jnp.where(swap, cols, rows)
        across = jnp.where(swap, rows, cols)
        address = (across >> 7) * BLK + down
        lanes = across & 127
        for s in range(STOPS):
            addr_v[s * LIST + k:s * LIST + k + 1, :] = address[s:s + 1, :]
            lane_v[s * LIST + k:s * LIST + k + 1, :] = lanes[s:s + 1, :]

    own_addr = pltpu.make_async_copy(addr_v.at[pl.ds(0, 4 * LIST)], addr_s.at[pl.ds(0, 4 * LIST)], addr_sem.at[0])
    own_addr.start()
    third_list = pl.ds(3 * LIST, LIST)
    asked_list = pl.ds(4 * LIST, LIST)
    ask = [
        pltpu.make_async_remote_copy(v.at[third_list], v.at[asked_list], ask_send.at[i], ask_recv.at[i],
                                     device_id=device(-1, 0, snp), device_id_type=MESH)
        for i, v in enumerate((addr_v, lane_v))
    ]

    @pl.when(even_core)
    def _():
        for copy in ask:
            copy.start()

    load_own.wait()
    own_addr.wait()

    lane_iota = lax.broadcasted_iota(jnp.int32, (8, 128), 1)
    sub_iota = lax.broadcasted_iota(jnp.int32, (8, 128), 0)
    tiles = (tile0, tile1)

    def multiply(lhs, rhs, tile, n):
        product = lax.dot_general(
            buf[lhs], buf[rhs, rows_of(n)], (((1,), (1,)), ((), ())), preferred_element_type=jnp.float32)
        tile[pl.ds(pl.multiple_of(n * 2 * BLK, BLK), BLK), :] = product[:, :128]
        tile[pl.ds(pl.multiple_of(n * 2 * BLK + BLK, BLK), BLK), :] = product[:, 128:]

    def read_out(tile, listed, into, n):
        group, first = n // 2, lax.rem(n, 2) * 64
        at = listed * LIST + group * 8
        lanes = lane_v[pl.ds(pl.multiple_of(at, 8), 8), :]
        slots = addr_s.at[pl.ds(at, 8)]
        found = jnp.zeros((8, 128), jnp.float32)
        for k in range(64):
            rows = None
            for s in range(8):
                one = jnp.broadcast_to(tile[pl.ds(slots[s, first + k], 1), :], (8, 128))
                rows = one if rows is None else jnp.where(sub_iota == s, one, rows)
            picked = jnp.take_along_axis(rows, lanes, axis=1)
            found = jnp.where(lane_iota == first + k, picked, found)
        here = pl.ds(pl.multiple_of(group * 8, 8), 8)
        mine = (lane_iota >= first) & (lane_iota < first + 64)
        sums[into, here, :] = jnp.where(mine, found, sums[into, here, :])

    def send_part(step, s, to, half, place):
        return pltpu.make_async_remote_copy(
            sums.at[step, pl.ds(pl.multiple_of(half * SHARE, SHARE), SHARE)], land.at[place, s],
            part_send.at[step, place], part_recv.at[place, s], device_id=to, device_id_type=MESH)

    def even_s(step):
        return (0, 1, 3, 2)[step]

    def send_sums(step):
        @pl.when(odd_core)
        def _():
            land[0, step] = sums[step, pl.ds(pl.multiple_of(snp * SHARE, SHARE), SHARE), :]
            send_part(step, step, partner, 1 - snp, 1).start()

        @pl.when(even_core)
        def _():
            s = even_s(step)
            if s == 3:
                send_part(step, 3, device(1, 0, snp), snp, 0).start()
                send_part(step, 3, device(1, 0, 1 - snp), 1 - snp, 1).start()
            else:
                land[0, s] = sums[step, pl.ds(pl.multiple_of(snp * SHARE, SHARE), SHARE), :]
                send_part(step, s, partner, 1 - snp, 1).start()

    for step in range(STOPS + 1):
        lhs = rhs = 0
        if step == 1:
            rhs = jnp.where(even_core, ODD, THIRD)
        elif step == 2:
            lhs = jnp.where(even_core, ODD, OWN)
            rhs = jnp.where(even_core, THIRD, ODD)
        elif step == 3:
            rhs = EVEN
        listed = step - 1
        if step == 3:
            listed = jnp.where(even_core, 4, 2)
        elif step == 4:
            listed = jnp.where(even_core, 2, 3)

        if step == 1:
            @pl.when(odd_core)
            def _():
                send_third(1).wait_recv()
        if step == 2:
            @pl.when(even_core)
            def _():
                send_third(0).wait_recv()
                for copy in ask:
                    copy.wait_recv()
                asked = pltpu.make_async_copy(addr_v.at[asked_list], addr_s.at[asked_list], addr_sem.at[1])
                asked.start()
                asked.wait()

        @pl.loop(0, CHUNKS)
        def _(n):
            if step == 1:
                @pl.when(even_core)
                def _():
                    send_odd(n).wait_recv()
                    pass_odd(n).start()

                @pl.when(even_core & (n == CHUNKS - 2))
                def _():
                    for m in range(CHUNKS):
                        send_even(m).start()
            if step == 2:
                @pl.when(odd_core)
                def _():
                    pass_odd(n).wait_recv()
            if step == 3:
                send_even(n).wait_recv()

                @pl.when(odd_core)
                def _():
                    pass_even(n).start()
            if step < STOPS:
                multiply(lhs, rhs, tiles[step % 2], n)
            if step > 0:
                read_out(tiles[(step - 1) % 2], listed, step - 1, n)
        if step > 0:
            send_sums(step - 1)

    @pl.when(odd_core)
    def _():
        for n in range(CHUNKS):
            send_odd(n).wait_send()
            pass_even(n).wait_send()
        for step in range(STOPS):
            send_part(step, step, partner, 1 - snp, 1).wait()

    @pl.when(even_core)
    def _():
        for n in range(CHUNKS):
            send_even(n).wait_send()
            pass_odd(n).wait_send()
        send_third(0).wait_send()
        send_third(1).wait_send()
        for copy in ask:
            copy.wait_send()
        for step in range(STOPS):
            s = even_s(step)
            if s == 3:
                send_part(step, 3, device(1, 0, snp), snp, 0).wait()
                send_part(step, 3, device(1, 0, 1 - snp), 1 - snp, 1).wait()
            else:
                send_part(step, s, partner, 1 - snp, 1).wait()

    for s in range(STOPS):
        both = land[0, s] + land[1, s]
        for k in range(SHARE):
            out[0, s:s + 1, k * 128:(k + 1) * 128] = both[k:k + 1, :]


def shards(dosage, pair_row, pair_col, pair_count):
    dma = pltpu.SemaphoreType.DMA
    sums = pl.pallas_call(
        kernel,
        out_shape=jax.ShapeDtypeStruct((1, STOPS, PAIRS // 2), jnp.float32),
        in_specs=[pl.BlockSpec(memory_space=pl.ANY)] * 3,
        out_specs=pl.BlockSpec(memory_space=pltpu.VMEM),
        scratch_shapes=[
            pltpu.VMEM((4, BLK, HALF), jnp.bfloat16),
            pltpu.VMEM((BLK * 16, 128), jnp.float32),
            pltpu.VMEM((BLK * 16, 128), jnp.float32),
            pltpu.VMEM((STOPS, PAIRS), jnp.int32),
            pltpu.VMEM((STOPS, PAIRS), jnp.int32),
            pltpu.VMEM((5 * LIST, 128), jnp.int32),
            pltpu.VMEM((5 * LIST, 128), jnp.int32),
            pltpu.SMEM((5 * LIST, 128), jnp.int32),
            pltpu.VMEM((STOPS, LIST, 128), jnp.float32),
            pltpu.VMEM((2, STOPS, SHARE, 128), jnp.float32),
            dma, dma((2,)), dma((2,)),
            dma((CHUNKS,)), dma((CHUNKS,)), dma((CHUNKS,)), dma((CHUNKS,)), dma((2,)), dma, dma((CHUNKS,)),
            dma((2,)), dma((2,)), dma((STOPS, 2)), dma((2, STOPS)),
        ],
        compiler_params=pltpu.CompilerParams(
            collective_id=0, has_side_effects=True, vmem_limit_bytes=56 << 20),
        cost_estimate=pl.CostEstimate(
            flops=2 * STOPS * BLK * BLK * HALF, bytes_accessed=2 * BLK * HALF * 2, transcendentals=0),
    )(dosage, pair_row, pair_col)
    slot = lax.axis_index("snp") * (PAIRS // 2) + jnp.arange(PAIRS // 2, dtype=jnp.int32)
    live = slot[None, None, :] < pair_count[:, :, None]
    return jnp.where(live, sums / SNPS, jnp.zeros_like(sums))


def solution(mesh):
    in_specs = (P("samp", "snp"), P("samp", None, None), P("samp", None, None), P("samp", None))
    out_specs = P("samp", None, "snp")
    return jax.shard_map(shards, mesh=mesh, in_specs=in_specs, out_specs=out_specs, check_vma=False)
```

```python
import jax
import jax.numpy as jnp
from jax import lax
from jax.experimental import pallas as pl
from jax.experimental.pallas import tpu as pltpu
from jax.sharding import PartitionSpec as P

MESH = pl.DeviceIdType.MESH

BLK = 2048
HALF = 512
QUARTER = 256
SNPS = 1024
STOPS = 4
PAIRS = 4096
CHIPS = 32
CHUNKS = 8
CHUNK = BLK // CHUNKS
LIST = PAIRS // 128
SHARE = LIST // 2
ROWS = LIST // CHUNKS
STEPS = 5
UNROLL = 2

OWN, LEFT, RIGHT, OTHER = 0, 1, 2, 3
LISTS = STOPS + 2


def kernel(x, row_hbm, col_hbm, out, buf, quart, own_quart, tile0, tile1, row_v, col_v, pair_v, addr_v, lane_v, slots0, slots1, sums, land,
           own_sem, list_sem, addr_sem, main_send, main_recv, pass_send, pass_recv, quart_send, quart_recv,
           sib_send, sib_recv, ask_send, ask_recv, part_send, part_recv):
    samp = lax.axis_index("samp")
    snp = lax.axis_index("snp")
    core = lax.rem(samp, 2)
    chip = samp // 2
    even_core = core == 0
    odd_core = core == 1

    def device(chip_step, to_core, to_snp):
        to_chip = lax.rem(chip + (chip_step + CHIPS), CHIPS)
        return {"samp": to_chip * 2 + to_core, "snp": to_snp}

    sibling = device(0, 1 - core, snp)
    ahead = 2 * core - 1
    main_to = device(ahead, 1 - core, snp)
    quart_to = device(-ahead, 1 - core, snp)

    barrier = pltpu.get_barrier_semaphore()
    greeted = [sibling, device(0, core, 1 - snp), device(0, 1 - core, 1 - snp)]
    for chip_step in (-1, 1):
        for to_core in (0, 1):
            for to_snp in (snp, 1 - snp):
                greeted.append(device(chip_step, to_core, to_snp))
    for other in greeted:
        pl.semaphore_signal(barrier, inc=1, device_id=other, device_id_type=MESH)
    pl.semaphore_wait(barrier, len(greeted))

    def rows_of(n):
        return pl.ds(pl.multiple_of(n * CHUNK, CHUNK), CHUNK)

    def send_main(n):
        return pltpu.make_async_remote_copy(
            x.at[rows_of(n)], buf.at[jnp.where(even_core, LEFT, RIGHT), rows_of(n)], main_send.at[n], main_recv.at[n],
            device_id=main_to, device_id_type=MESH)

    def pass_on(n):
        return pltpu.make_async_remote_copy(
            buf.at[RIGHT, rows_of(n)], buf.at[RIGHT, rows_of(n)], pass_send.at[n], pass_recv.at[n],
            device_id=sibling, device_id_type=MESH)

    def send_quarter(n):
        columns = pl.ds(pl.multiple_of(core * QUARTER, QUARTER), QUARTER)
        return pltpu.make_async_remote_copy(
            x.at[rows_of(n), columns], quart.at[rows_of(n)], quart_send.at[n], quart_recv.at[n],
            device_id=quart_to, device_id_type=MESH)

    send_sib = pltpu.make_async_remote_copy(
        x, buf.at[jnp.where(even_core, OTHER, LEFT)], sib_send, sib_recv, device_id=sibling, device_id_type=MESH)

    load_own = pltpu.make_async_copy(x, buf.at[OWN], own_sem)
    load_row = pltpu.make_async_copy(row_hbm.at[0], row_v, list_sem.at[0])
    load_col = pltpu.make_async_copy(col_hbm.at[0], col_v, list_sem.at[1])
    load_part = pltpu.make_async_copy(
        x.at[:, pl.ds(pl.multiple_of((1 - core) * QUARTER, QUARTER), QUARTER)], own_quart, list_sem.at[2])
    load_own.start()
    send_sib.start()
    for n in range(CHUNKS):
        send_main(n).start()
    load_row.start()
    load_col.start()
    load_part.start()
    def ask(i):
        to = device(-1, 1 - core, snp) if i == 1 else device(core - 1, 1 - core, snp)
        return pltpu.make_async_remote_copy(
            pair_v.at[pl.ds((2 + i) * LIST, LIST)], pair_v.at[pl.ds((4 + i) * LIST, LIST)], ask_send.at[i], ask_recv.at[i],
            device_id=to, device_id_type=MESH)

    slots = (slots0, slots1)

    def load_slots(step):
        return pltpu.make_async_copy(
            addr_v.at[pl.ds(step * LIST, UNROLL * ROWS)], slots[step % 2], addr_sem.at[step % 2, 0])

    def reload_slots(step, m, n):
        return pltpu.make_async_copy(
            addr_v.at[pl.ds(step * LIST + ((m + 1) * UNROLL + n) * ROWS, ROWS)], slots[step % 2].at[pl.ds(n * ROWS, ROWS)],
            addr_sem.at[step % 2, 1 + n])

    def prepare(step):
        listed = (0, 0, jnp.where(even_core, 1, 4), jnp.where(even_core, 4, 5), jnp.where(even_core, 5, 3))[step]
        if step == 1:
            listed = jnp.where(even_core, 0, 1)
        swapped = {2: odd_core, 4: even_core}.get(step)
        for group in range(LIST // 8):
            pairs = pair_v[pl.ds(pl.multiple_of(listed * LIST + group * 8, 8), 8), :]
            down, across = pairs >> 11, pairs & (BLK - 1)
            if swapped is not None:
                swap = jnp.broadcast_to(swapped, (8, 128))
                down, across = jnp.where(swap, across, down), jnp.where(swap, down, across)
            here = slice(step * LIST + group * 8, step * LIST + group * 8 + 8)
            addr_v[here, :] = (across >> 7) * BLK + down
            lanes = across & 127
            turned = pltpu.roll(lanes, 64, 1)
            at = (step * LIST + group * 8) * 2
            for i in range(2):
                lane_v[at + 8 * i:at + 8 * i + 4, :] = lanes[4 * i:4 * i + 4, :]
                lane_v[at + 8 * i + 4:at + 8 * i + 8, :] = turned[4 * i:4 * i + 4, :]


    def read_lists():
        load_row.wait()
        load_col.wait()

        for k in range(LIST):
            pairs = row_v[:, k * 128:(k + 1) * 128] * BLK + col_v[:, k * 128:(k + 1) * 128]
            for s in range(STOPS):
                pair_v[s * LIST + k:s * LIST + k + 1, :] = pairs[s:s + 1, :]
        ask(0).start()
        ask(1).start()
        prepare(0)
        load_slots(0).start()
        prepare(1)

    load_own.wait()

    lane_iota = lax.broadcasted_iota(jnp.int32, (8, 128), 1)
    sub_iota = lax.broadcasted_iota(jnp.int32, (8, 128), 0)
    tiles = (tile0, tile1)

    def multiply(step, n, on_core=None):
        tile = tiles[step % 2]
        if step == 0:
            lhs, rhs = buf[OWN], buf[OWN, rows_of(n)]
        elif step == 1:
            lhs, rhs = buf[OWN], buf[OTHER, rows_of(n)]
        elif step == 2 and on_core == 0:
            lhs, rhs = buf[OWN], buf[RIGHT, rows_of(n)]
        elif step == 2:
            lhs, rhs = buf[OTHER], buf[LEFT, rows_of(n)]
        elif step == 3:
            lhs, rhs = buf[LEFT], buf[RIGHT, rows_of(n)]
        else:
            lhs, rhs = own_quart[...], quart[rows_of(n)]
        product = lax.dot_general(lhs, rhs, (((1,), (1,)), ((), ())), preferred_element_type=jnp.float32)
        tile[pl.ds(pl.multiple_of(n * 2 * BLK, BLK), BLK), :] = product[:, :128]
        tile[pl.ds(pl.multiple_of(n * 2 * BLK + BLK, BLK), BLK), :] = product[:, 128:]

    def read_out(step, n, q):
        tile, here = tiles[step % 2], slots[step % 2]
        lanes = lane_v[pl.ds(pl.multiple_of(step * LIST * 2 + n * 8, 8), 8), :]
        found = jnp.zeros((8, 128), jnp.float32)
        for k in range(64):
            rows = None
            for s in range(8):
                at = here[q * ROWS + s % ROWS, s // ROWS * 64 + k]
                one = jnp.broadcast_to(tile[pl.ds(at, 1), :], (8, 128))
                rows = one if rows is None else jnp.where(sub_iota == s, one, rows)
            picked = jnp.take_along_axis(rows, lanes, axis=1)
            found = jnp.where(lane_iota == k, picked, found)
        turned = pltpu.roll(found, 64, 1)
        sums[step, pl.ds(n * ROWS, ROWS), :] = jnp.where(lane_iota[:ROWS] < 64, found[:ROWS], turned[ROWS:])

    def share(step, half):
        return sums.at[step, pl.ds(pl.multiple_of(half * SHARE, SHARE), SHARE)]

    def send_part(step, half, to, place, s):
        return pltpu.make_async_remote_copy(
            share(step, half), land.at[place, s], part_send.at[step, place % 2], part_recv.at[place, s],
            device_id=to, device_id_type=MESH)

    even_parts = {0: (0, 0, None, 0), 2: (1, 0, None, 0), 3: (2, 0, 1, 0), 4: (3, 1, 1, 2)}
    odd_parts = {0: (0, 0, None, 0), 1: (1, 0, None, 0), 2: (2, 1, 0, 0), 3: (3, 1, 0, 0), 4: (3, 0, None, 0)}

    def part_copies(step, parts):
        s, chip_step, to_core, place = parts[step]
        if to_core is None:
            return [send_part(step, 1 - snp, device(0, core, 1 - snp), 1, s)]
        return [send_part(step, snp, device(chip_step, to_core, snp), place, s),
                send_part(step, 1 - snp, device(chip_step, to_core, 1 - snp), place + 1, s)]

    def hand_out(step):
        for own, parts in ((even_core, even_parts), (odd_core, odd_parts)):
            if step in parts:
                @pl.when(own)
                def _():
                    for copy in part_copies(step, parts):
                        copy.start()
                    if parts[step][2] is None:
                        land[0, parts[step][0]] = share(step, snp)[...]

    for step in range(STEPS + 1):
        if step == 1:
            read_lists()
            send_sib.wait_recv()
        if step == 2:
            ask(0).wait_recv()
            ask(1).wait_recv()
            for later in range(2, STEPS):
                prepare(later)
            for n in range(CHUNKS - 2):
                send_main(n).wait_send()
            for n in range(CHUNKS // 2):
                send_quarter(n).start()
        if step == 4:
            load_part.wait()
        if step > 0:
            load_slots(step - 1).wait()
        if 0 < step < STEPS:
            load_slots(step).start()

        @pl.loop(0, CHUNKS // UNROLL)
        def _(m):
            for q in range(UNROLL):
                n = m * UNROLL + q
                if step == 2:
                    send_main(n).wait_recv()

                    @pl.when(even_core)
                    def _():
                        pass_on(n).start()

                    if q == 0:
                        @pl.when(n == CHUNKS - UNROLL)
                        def _():
                            for i in range(CHUNKS // 2, CHUNKS):
                                send_quarter(i).start()
                if step == 3:
                    @pl.when(odd_core)
                    def _():
                        pass_on(n).wait_recv()
                if step == 4:
                    send_quarter(n).wait_recv()
                if step > 0:
                    @pl.when(m > 0)
                    def _():
                        reload_slots(step - 1, m - 1, q).wait()

                if step == 1:
                    @pl.when(odd_core)
                    def _():
                        multiply(step, n)
                        read_out(step - 1, n, q)

                    @pl.when(even_core)
                    def _():
                        read_out(step - 1, n, q)
                elif step == 2:
                    @pl.when(odd_core)
                    def _():
                        multiply(step, n)
                        read_out(step - 1, n, q)

                    @pl.when(even_core)
                    def _():
                        multiply(step, n, 0)
                elif 0 < step < STEPS:
                    @pl.when(core < 2)
                    def _():
                        multiply(step, n)
                        read_out(step - 1, n, q)
                elif step == 0:
                    multiply(step, n)
                else:
                    read_out(step - 1, n, q)

                if step > 0:
                    @pl.when(m < CHUNKS // UNROLL - 1)
                    def _():
                        reload_slots(step - 1, m, q).start()
        if step > 0:
            hand_out(step - 1)

    for n in range(CHUNKS):
        if n >= CHUNKS - 2:
            send_main(n).wait_send()
        send_quarter(n).wait_send()
    send_sib.wait_send()
    ask(0).wait_send()
    ask(1).wait_send()

    def landed(place, s):
        send_part(0, snp, sibling, place, s).wait_recv()

    for own, parts in ((even_core, even_parts), (odd_core, odd_parts)):
        @pl.when(own)
        def _():
            for step in parts:
                for copy in part_copies(step, parts):
                    copy.wait_send()
    for s in range(STOPS):
        landed(1, s)
    landed(0, 2)

    @pl.when(even_core)
    def _():
        for n in range(CHUNKS):
            pass_on(n).wait_send()
        landed(0, 3)

    @pl.when(odd_core)
    def _():
        landed(2, 3)
        landed(3, 3)
        land[0, 3] = land[0, 3] + (land[2, 3] + land[3, 3])

    for s in range(STOPS):
        both = land[0, s] + land[1, s]
        for k in range(SHARE):
            out[0, s:s + 1, k * 128:(k + 1) * 128] = both[k:k + 1, :]


def shards(dosage, pair_row, pair_col, pair_count):
    dma = pltpu.SemaphoreType.DMA
    sums = pl.pallas_call(
        kernel,
        out_shape=jax.ShapeDtypeStruct((1, STOPS, PAIRS // 2), jnp.float32),
        in_specs=[pl.BlockSpec(memory_space=pl.ANY)] * 3,
        out_specs=pl.BlockSpec(memory_space=pltpu.VMEM),
        scratch_shapes=[
            pltpu.VMEM((4, BLK, HALF), jnp.bfloat16),
            pltpu.VMEM((BLK, QUARTER), jnp.bfloat16),
            pltpu.VMEM((BLK, QUARTER), jnp.bfloat16),
            pltpu.VMEM((BLK * 16, 128), jnp.float32),
            pltpu.VMEM((BLK * 16, 128), jnp.float32),
            pltpu.VMEM((STOPS, PAIRS), jnp.int32),
            pltpu.VMEM((STOPS, PAIRS), jnp.int32),
            pltpu.VMEM((LISTS * LIST, 128), jnp.int32),
            pltpu.VMEM((STEPS * LIST, 128), jnp.int32),
            pltpu.VMEM((STEPS * LIST * 2, 128), jnp.int32),
            pltpu.SMEM((UNROLL * ROWS, 128), jnp.int32),
            pltpu.SMEM((UNROLL * ROWS, 128), jnp.int32),
            pltpu.VMEM((STEPS, LIST, 128), jnp.float32),
            pltpu.VMEM((4, STOPS, SHARE, 128), jnp.float32),
            dma, dma((3,)), dma((2, 1 + UNROLL)),
            dma((CHUNKS,)), dma((CHUNKS,)), dma((CHUNKS,)), dma((CHUNKS,)), dma((CHUNKS,)), dma((CHUNKS,)),
            dma, dma, dma((2,)), dma((2,)), dma((STEPS, 2)), dma((4, STOPS)),
        ],
        compiler_params=pltpu.CompilerParams(
            collective_id=0, has_side_effects=True, vmem_limit_bytes=56 << 20),
        cost_estimate=pl.CostEstimate(
            flops=2 * STOPS * BLK * BLK * HALF, bytes_accessed=2 * BLK * HALF * 2, transcendentals=0),
    )(dosage, pair_row, pair_col)
    slot = lax.axis_index("snp") * (PAIRS // 2) + jnp.arange(PAIRS // 2, dtype=jnp.int32)
    live = slot[None, None, :] < pair_count[:, :, None]
    return jnp.where(live, sums / SNPS, jnp.zeros_like(sums))


def solution(mesh):
    in_specs = (P("samp", "snp"), P("samp", None, None), P("samp", None, None), P("samp", None))
    out_specs = P("samp", None, "snp")
    return jax.shard_map(shards, mesh=mesh, in_specs=in_specs, out_specs=out_specs, check_vma=False)
```

```python
import jax
import jax.numpy as jnp
from jax import lax
from jax.experimental import pallas as pl
from jax.experimental.pallas import tpu as pltpu
from jax.sharding import PartitionSpec as P

MESH = pl.DeviceIdType.MESH

BLK = 2048
HALF = 512
QUARTER = 256
SNPS = 1024
STOPS = 4
PAIRS = 4096
CHIPS = 32
CHUNKS = 8
CHUNK = BLK // CHUNKS
LIST = PAIRS // 128
SHARE = LIST // 2
ROWS = LIST // CHUNKS
STEPS = 5
FIRST = 5
UNROLL = 2

OWN, LEFT, RIGHT, OTHER = 0, 1, 2, 3
LISTS = STOPS + 2


def kernel(x, row_hbm, col_hbm, out, buf, quart, own_quart, tile0, tile1, row_v, col_v, pair_v, addr_v, lane_v, slots0, slots1, sums, land,
           own_sem, list_sem, addr_sem, main_send, main_recv, pass_send, pass_recv, quart_send, quart_recv,
           sib_send, sib_recv, ask_send, ask_recv, part_send, part_recv):
    samp = lax.axis_index("samp")
    snp = lax.axis_index("snp")
    core = lax.rem(samp, 2)
    chip = samp // 2
    even_core = core == 0
    odd_core = core == 1

    def device(chip_step, to_core, to_snp):
        to_chip = lax.rem(chip + (chip_step + CHIPS), CHIPS)
        return {"samp": to_chip * 2 + to_core, "snp": to_snp}

    sibling = device(0, 1 - core, snp)
    ahead = 2 * core - 1
    main_to = device(ahead, 1 - core, snp)
    quart_to = device(-ahead, 1 - core, snp)

    barrier = pltpu.get_barrier_semaphore()
    greeted = [sibling, device(0, core, 1 - snp), device(0, 1 - core, 1 - snp)]
    for chip_step in (-1, 1):
        for to_core in (0, 1):
            for to_snp in (snp, 1 - snp):
                greeted.append(device(chip_step, to_core, to_snp))
    for other in greeted:
        pl.semaphore_signal(barrier, inc=1, device_id=other, device_id_type=MESH)
    pl.semaphore_wait(barrier, len(greeted))

    def rows_of(n):
        return pl.ds(pl.multiple_of(n * CHUNK, CHUNK), CHUNK)

    def send_main(n):
        return pltpu.make_async_remote_copy(
            x.at[rows_of(n)], buf.at[jnp.where(even_core, LEFT, RIGHT), rows_of(n)], main_send.at[n], main_recv.at[n],
            device_id=main_to, device_id_type=MESH)

    def pass_on(n):
        return pltpu.make_async_remote_copy(
            buf.at[RIGHT, rows_of(n)], buf.at[RIGHT, rows_of(n)], pass_send.at[n], pass_recv.at[n],
            device_id=sibling, device_id_type=MESH)

    def send_quarter(n):
        columns = pl.ds(pl.multiple_of(core * QUARTER, QUARTER), QUARTER)
        return pltpu.make_async_remote_copy(
            x.at[rows_of(n), columns], quart.at[rows_of(n)], quart_send.at[n], quart_recv.at[n],
            device_id=quart_to, device_id_type=MESH)

    send_sib = pltpu.make_async_remote_copy(
        x, buf.at[jnp.where(even_core, OTHER, LEFT)], sib_send, sib_recv, device_id=sibling, device_id_type=MESH)

    load_own = pltpu.make_async_copy(x, buf.at[OWN], own_sem)
    load_row = pltpu.make_async_copy(row_hbm.at[0], row_v, list_sem.at[0])
    load_col = pltpu.make_async_copy(col_hbm.at[0], col_v, list_sem.at[1])
    load_part = pltpu.make_async_copy(
        x.at[:, pl.ds(pl.multiple_of((1 - core) * QUARTER, QUARTER), QUARTER)], own_quart, list_sem.at[2])
    load_own.start()
    send_sib.start()
    for n in range(FIRST):
        send_main(n).start()
    load_row.start()
    load_col.start()
    load_part.start()
    def ask(i):
        to = device(-1, 1 - core, snp) if i == 1 else device(core - 1, 1 - core, snp)
        return pltpu.make_async_remote_copy(
            pair_v.at[pl.ds((2 + i) * LIST, LIST)], pair_v.at[pl.ds((4 + i) * LIST, LIST)], ask_send.at[i], ask_recv.at[i],
            device_id=to, device_id_type=MESH)

    slots = (slots0, slots1)

    def load_slots(step):
        return pltpu.make_async_copy(
            addr_v.at[pl.ds(step * LIST, UNROLL * ROWS)], slots[step % 2].at[pl.ds(0, UNROLL * ROWS)], addr_sem.at[step % 2, 0])

    def load_all_slots(step):
        return pltpu.make_async_copy(addr_v.at[pl.ds(step * LIST, LIST)], slots[step % 2], addr_sem.at[step % 2, 0])

    def reload_slots(step, m, n):
        return pltpu.make_async_copy(
            addr_v.at[pl.ds(step * LIST + ((m + 1) * UNROLL + n) * ROWS, ROWS)], slots[step % 2].at[pl.ds(n * ROWS, ROWS)],
            addr_sem.at[step % 2, 1 + n])

    def prepare(step):
        listed = (0, 0, jnp.where(even_core, 1, 4), jnp.where(even_core, 4, 5), jnp.where(even_core, 5, 3))[step]
        if step == 1:
            listed = jnp.where(even_core, 0, 1)
        swapped = {2: odd_core, 4: even_core}.get(step)
        for group in range(LIST // 8):
            pairs = pair_v[pl.ds(pl.multiple_of(listed * LIST + group * 8, 8), 8), :]
            down, across = pairs >> 11, pairs & (BLK - 1)
            if swapped is not None:
                swap = jnp.broadcast_to(swapped, (8, 128))
                down, across = jnp.where(swap, across, down), jnp.where(swap, down, across)
            here = slice(step * LIST + group * 8, step * LIST + group * 8 + 8)
            addr_v[here, :] = (across >> 7) * BLK + down
            lanes = across & 127
            turned = pltpu.roll(lanes, 64, 1)
            at = (step * LIST + group * 8) * 2
            for i in range(2):
                lane_v[at + 8 * i:at + 8 * i + 4, :] = lanes[4 * i:4 * i + 4, :]
                lane_v[at + 8 * i + 4:at + 8 * i + 8, :] = turned[4 * i:4 * i + 4, :]


    def read_lists():
        load_row.wait()
        load_col.wait()

        for k in range(LIST):
            pairs = row_v[:, k * 128:(k + 1) * 128] * BLK + col_v[:, k * 128:(k + 1) * 128]
            for s in range(STOPS):
                pair_v[s * LIST + k:s * LIST + k + 1, :] = pairs[s:s + 1, :]
        ask(0).start()
        ask(1).start()
        for n in range(FIRST, CHUNKS):
            send_main(n).start()
        prepare(0)
        load_slots(0).start()
        prepare(1)

    load_own.wait()

    lane_iota = lax.broadcasted_iota(jnp.int32, (8, 128), 1)
    sub_iota = lax.broadcasted_iota(jnp.int32, (8, 128), 0)
    tiles = (tile0, tile1)

    def multiply(step, n, on_core=None):
        tile = tiles[step % 2]
        if step == 0:
            lhs, rhs = buf[OWN], buf[OWN, rows_of(n)]
        elif step == 1:
            lhs, rhs = buf[OWN], buf[OTHER, rows_of(n)]
        elif step == 2 and on_core == 0:
            lhs, rhs = buf[OWN], buf[RIGHT, rows_of(n)]
        elif step == 2:
            lhs, rhs = buf[OTHER], buf[LEFT, rows_of(n)]
        elif step == 3:
            lhs, rhs = buf[LEFT], buf[RIGHT, rows_of(n)]
        else:
            lhs, rhs = own_quart[...], quart[rows_of(n)]
        product = lax.dot_general(lhs, rhs, (((1,), (1,)), ((), ())), preferred_element_type=jnp.float32)
        tile[pl.ds(pl.multiple_of(n * 2 * BLK, BLK), BLK), :] = product[:, :128]
        tile[pl.ds(pl.multiple_of(n * 2 * BLK + BLK, BLK), BLK), :] = product[:, 128:]

    def read_out(step, n, q):
        tile, here = tiles[step % 2], slots[step % 2]
        lanes = lane_v[pl.ds(pl.multiple_of(step * LIST * 2 + n * 8, 8), 8), :]
        found = jnp.zeros((8, 128), jnp.float32)
        for k in range(64):
            rows = None
            for s in range(8):
                at = here[q * ROWS + s % ROWS, s // ROWS * 64 + k]
                one = jnp.broadcast_to(tile[pl.ds(at, 1), :], (8, 128))
                rows = one if rows is None else jnp.where(sub_iota == s, one, rows)
            picked = jnp.take_along_axis(rows, lanes, axis=1)
            found = jnp.where(lane_iota == k, picked, found)
        turned = pltpu.roll(found, 64, 1)
        sums[step, pl.ds(n * ROWS, ROWS), :] = jnp.where(lane_iota[:ROWS] < 64, found[:ROWS], turned[ROWS:])

    def share(step, half):
        return sums.at[step, pl.ds(pl.multiple_of(half * SHARE, SHARE), SHARE)]

    def send_part(step, half, to, place, s):
        return pltpu.make_async_remote_copy(
            share(step, half), land.at[place, s], part_send.at[step, place % 2], part_recv.at[place, s],
            device_id=to, device_id_type=MESH)

    even_parts = {0: (0, 0, None, 0), 2: (1, 0, None, 0), 3: (2, 0, 1, 0), 4: (3, 1, 1, 2)}
    odd_parts = {0: (0, 0, None, 0), 1: (1, 0, None, 0), 2: (2, 1, 0, 0), 3: (3, 1, 0, 0), 4: (3, 0, None, 0)}

    def part_copies(step, parts):
        s, chip_step, to_core, place = parts[step]
        if to_core is None:
            return [send_part(step, 1 - snp, device(0, core, 1 - snp), 1, s)]
        return [send_part(step, snp, device(chip_step, to_core, snp), place, s),
                send_part(step, 1 - snp, device(chip_step, to_core, 1 - snp), place + 1, s)]

    def hand_out(step):
        for own, parts in ((even_core, even_parts), (odd_core, odd_parts)):
            if step in parts:
                @pl.when(own)
                def _():
                    for copy in part_copies(step, parts):
                        copy.start()
                    if parts[step][2] is None:
                        land[0, parts[step][0]] = share(step, snp)[...]

    for step in range(STEPS - 1):
        if step == 1:
            read_lists()
            send_sib.wait_recv()
        if step == 2:
            ask(0).wait_recv()
            ask(1).wait_recv()
            for later in range(2, STEPS):
                prepare(later)
            for n in range(CHUNKS - 2):
                send_main(n).wait_send()
            for n in range(CHUNKS // 2):
                send_quarter(n).start()
        if step > 0:
            load_slots(step - 1).wait()
        if 0 < step < 3:
            load_slots(step).start()
        if step == 3:
            load_all_slots(3).start()

        @pl.loop(0, CHUNKS // UNROLL)
        def _(m):
            for q in range(UNROLL):
                n = m * UNROLL + q
                if step == 2:
                    send_main(n).wait_recv()

                    @pl.when(even_core)
                    def _():
                        pass_on(n).start()

                    if q == 0:
                        @pl.when(n == CHUNKS - UNROLL)
                        def _():
                            for i in range(CHUNKS // 2, CHUNKS):
                                send_quarter(i).start()
                if step == 3:
                    @pl.when(odd_core)
                    def _():
                        pass_on(n).wait_recv()
                if step > 0:
                    @pl.when(m > 0)
                    def _():
                        reload_slots(step - 1, m - 1, q).wait()

                if step == 1:
                    @pl.when(odd_core)
                    def _():
                        multiply(step, n)
                        read_out(step - 1, n, q)

                    @pl.when(even_core)
                    def _():
                        read_out(step - 1, n, q)
                elif step == 2:
                    @pl.when(odd_core)
                    def _():
                        multiply(step, n)
                        read_out(step - 1, n, q)

                    @pl.when(even_core)
                    def _():
                        multiply(step, n, 0)
                elif step == 3:
                    @pl.when(core < 2)
                    def _():
                        multiply(step, n)
                        read_out(step - 1, n, q)
                else:
                    multiply(step, n)

                if step > 0:
                    @pl.when(m < CHUNKS // UNROLL - 1)
                    def _():
                        reload_slots(step - 1, m, q).start()
        if step > 0:
            hand_out(step - 1)

    load_all_slots(4).start()
    load_all_slots(3).wait()
    for n in range(CHUNKS):
        read_out(3, n, n)
    hand_out(3)
    load_part.wait()

    @pl.loop(0, CHUNKS // UNROLL)
    def _(m):
        for q in range(UNROLL):
            send_quarter(m * UNROLL + q).wait_recv()
            multiply(4, m * UNROLL + q)

    load_all_slots(4).wait()
    for n in range(CHUNKS):
        read_out(4, n, n)
    hand_out(4)

    for n in range(CHUNKS):
        if n >= CHUNKS - 2:
            send_main(n).wait_send()
        send_quarter(n).wait_send()
    send_sib.wait_send()
    ask(0).wait_send()
    ask(1).wait_send()

    def landed(place, s):
        send_part(0, snp, sibling, place, s).wait_recv()

    for own, parts in ((even_core, even_parts), (odd_core, odd_parts)):
        @pl.when(own)
        def _():
            for step in parts:
                for copy in part_copies(step, parts):
                    copy.wait_send()
    for s in range(STOPS):
        landed(1, s)
    landed(0, 2)

    @pl.when(even_core)
    def _():
        for n in range(CHUNKS):
            pass_on(n).wait_send()
        landed(0, 3)

    @pl.when(odd_core)
    def _():
        landed(2, 3)
        landed(3, 3)
        land[0, 3] = land[0, 3] + (land[2, 3] + land[3, 3])

    for s in range(STOPS):
        both = land[0, s] + land[1, s]
        for k in range(SHARE):
            out[0, s:s + 1, k * 128:(k + 1) * 128] = both[k:k + 1, :]


def shards(dosage, pair_row, pair_col, pair_count):
    dma = pltpu.SemaphoreType.DMA
    sums = pl.pallas_call(
        kernel,
        out_shape=jax.ShapeDtypeStruct((1, STOPS, PAIRS // 2), jnp.float32),
        in_specs=[pl.BlockSpec(memory_space=pl.ANY)] * 3,
        out_specs=pl.BlockSpec(memory_space=pltpu.VMEM),
        scratch_shapes=[
            pltpu.VMEM((4, BLK, HALF), jnp.bfloat16),
            pltpu.VMEM((BLK, QUARTER), jnp.bfloat16),
            pltpu.VMEM((BLK, QUARTER), jnp.bfloat16),
            pltpu.VMEM((BLK * 16, 128), jnp.float32),
            pltpu.VMEM((BLK * 16, 128), jnp.float32),
            pltpu.VMEM((STOPS, PAIRS), jnp.int32),
            pltpu.VMEM((STOPS, PAIRS), jnp.int32),
            pltpu.VMEM((LISTS * LIST, 128), jnp.int32),
            pltpu.VMEM((STEPS * LIST, 128), jnp.int32),
            pltpu.VMEM((STEPS * LIST * 2, 128), jnp.int32),
            pltpu.SMEM((LIST, 128), jnp.int32),
            pltpu.SMEM((LIST, 128), jnp.int32),
            pltpu.VMEM((STEPS, LIST, 128), jnp.float32),
            pltpu.VMEM((4, STOPS, SHARE, 128), jnp.float32),
            dma, dma((3,)), dma((2, 1 + UNROLL)),
            dma((CHUNKS,)), dma((CHUNKS,)), dma((CHUNKS,)), dma((CHUNKS,)), dma((CHUNKS,)), dma((CHUNKS,)),
            dma, dma, dma((2,)), dma((2,)), dma((STEPS, 2)), dma((4, STOPS)),
        ],
        compiler_params=pltpu.CompilerParams(
            collective_id=0, has_side_effects=True, vmem_limit_bytes=56 << 20),
        cost_estimate=pl.CostEstimate(
            flops=2 * STOPS * BLK * BLK * HALF, bytes_accessed=2 * BLK * HALF * 2, transcendentals=0),
    )(dosage, pair_row, pair_col)
    slot = lax.axis_index("snp") * (PAIRS // 2) + jnp.arange(PAIRS // 2, dtype=jnp.int32)
    live = slot[None, None, :] < pair_count[:, :, None]
    return jnp.where(live, sums / SNPS, jnp.zeros_like(sums))


def solution(mesh):
    in_specs = (P("samp", "snp"), P("samp", None, None), P("samp", None, None), P("samp", None))
    out_specs = P("samp", None, "snp")
    return jax.shard_map(shards, mesh=mesh, in_specs=in_specs, out_specs=out_specs, check_vma=False)
```

```python
import jax
import jax.numpy as jnp
from jax import lax
from jax.experimental import pallas as pl
from jax.experimental.pallas import tpu as pltpu
from jax.sharding import PartitionSpec as P

MESH = pl.DeviceIdType.MESH

BLK = 2048
HALF = 512
QUARTER = 256
SNPS = 1024
STOPS = 4
PAIRS = 4096
CHIPS = 32
CHUNKS = 8
CHUNK = BLK // CHUNKS
LIST = PAIRS // 128
SHARE = LIST // 2
ROWS = LIST // CHUNKS
STEPS = 5
FIRST = 5
UNROLL = 2

OWN, LEFT, RIGHT, OTHER = 0, 1, 2, 3
LISTS = STOPS + 2


def kernel(x, row_hbm, col_hbm, out, buf, quart, own_quart, tile0, tile1, row_v, col_v, pair_v, addr_v, lane_v, slots0, slots1, sums, land,
           own_sem, list_sem, addr_sem, main_send, main_recv, pass_send, pass_recv, quart_send, quart_recv,
           sib_send, sib_recv, ask_send, ask_recv, part_send, part_recv):
    samp = lax.axis_index("samp")
    snp = lax.axis_index("snp")
    core = lax.rem(samp, 2)
    chip = samp // 2
    even_core = core == 0
    odd_core = core == 1

    def device(chip_step, to_core, to_snp):
        to_chip = lax.rem(chip + (chip_step + CHIPS), CHIPS)
        return {"samp": to_chip * 2 + to_core, "snp": to_snp}

    sibling = device(0, 1 - core, snp)
    ahead = 2 * core - 1
    main_to = device(ahead, 1 - core, snp)
    quart_to = device(-ahead, 1 - core, snp)

    barrier = pltpu.get_barrier_semaphore()
    greeted = [sibling, device(0, core, 1 - snp), device(0, 1 - core, 1 - snp)]
    for chip_step in (-1, 1):
        for to_core in (0, 1):
            for to_snp in (snp, 1 - snp):
                greeted.append(device(chip_step, to_core, to_snp))
    for other in greeted:
        pl.semaphore_signal(barrier, inc=1, device_id=other, device_id_type=MESH)
    pl.semaphore_wait(barrier, len(greeted))

    def rows_of(n):
        return pl.ds(pl.multiple_of(n * CHUNK, CHUNK), CHUNK)

    def send_main(n):
        return pltpu.make_async_remote_copy(
            x.at[rows_of(n)], buf.at[jnp.where(even_core, LEFT, RIGHT), rows_of(n)], main_send.at[n], main_recv.at[n],
            device_id=main_to, device_id_type=MESH)

    def pass_on(n):
        return pltpu.make_async_remote_copy(
            buf.at[RIGHT, rows_of(n)], buf.at[RIGHT, rows_of(n)], pass_send.at[n], pass_recv.at[n],
            device_id=sibling, device_id_type=MESH)

    def send_quarter(n):
        columns = pl.ds(pl.multiple_of(core * QUARTER, QUARTER), QUARTER)
        return pltpu.make_async_remote_copy(
            x.at[rows_of(n), columns], quart.at[rows_of(n)], quart_send.at[n], quart_recv.at[n],
            device_id=quart_to, device_id_type=MESH)

    send_sib = pltpu.make_async_remote_copy(
        x, buf.at[jnp.where(even_core, OTHER, LEFT)], sib_send, sib_recv, device_id=sibling, device_id_type=MESH)

    load_own = pltpu.make_async_copy(x, buf.at[OWN], own_sem)
    load_row = pltpu.make_async_copy(row_hbm.at[0], row_v, list_sem.at[0])
    load_col = pltpu.make_async_copy(col_hbm.at[0], col_v, list_sem.at[1])
    load_part = pltpu.make_async_copy(
        x.at[:, pl.ds(pl.multiple_of((1 - core) * QUARTER, QUARTER), QUARTER)], own_quart, list_sem.at[2])
    load_own.start()
    send_sib.start()
    for n in range(FIRST):
        send_main(n).start()
    load_row.start()
    load_col.start()
    load_part.start()
    def ask(i):
        to = device(-1, 1 - core, snp) if i == 1 else device(core - 1, 1 - core, snp)
        return pltpu.make_async_remote_copy(
            pair_v.at[pl.ds((2 + i) * LIST, LIST)], pair_v.at[pl.ds((4 + i) * LIST, LIST)], ask_send.at[i], ask_recv.at[i],
            device_id=to, device_id_type=MESH)

    slots = (slots0, slots1)

    def load_slots(step):
        return pltpu.make_async_copy(
            addr_v.at[pl.ds(step * LIST, UNROLL * ROWS)], slots[step % 2].at[pl.ds(0, UNROLL * ROWS)], addr_sem.at[step % 2, 0])

    def load_all_slots(step):
        return pltpu.make_async_copy(addr_v.at[pl.ds(step * LIST, LIST)], slots[step % 2], addr_sem.at[step % 2, 0])

    def reload_slots(step, m, n):
        return pltpu.make_async_copy(
            addr_v.at[pl.ds(step * LIST + ((m + 1) * UNROLL + n) * ROWS, ROWS)], slots[step % 2].at[pl.ds(n * ROWS, ROWS)],
            addr_sem.at[step % 2, 1 + n])

    def prepare(step):
        listed = (0, 0, jnp.where(even_core, 1, 4), jnp.where(even_core, 4, 5), jnp.where(even_core, 5, 3))[step]
        if step == 1:
            listed = jnp.where(even_core, 0, 1)
        swapped = {2: odd_core, 4: even_core}.get(step)
        for group in range(LIST // 8):
            pairs = pair_v[pl.ds(pl.multiple_of(listed * LIST + group * 8, 8), 8), :]
            down, across = pairs >> 11, pairs & (BLK - 1)
            if swapped is not None:
                swap = jnp.broadcast_to(swapped, (8, 128))
                down, across = jnp.where(swap, across, down), jnp.where(swap, down, across)
            here = slice(step * LIST + group * 8, step * LIST + group * 8 + 8)
            addr_v[here, :] = (across >> 7) * BLK + down
            lanes = across & 127
            turned = pltpu.roll(lanes, 64, 1)
            at = (step * LIST + group * 8) * 2
            for i in range(2):
                lane_v[at + 8 * i:at + 8 * i + 4, :] = lanes[4 * i:4 * i + 4, :]
                lane_v[at + 8 * i + 4:at + 8 * i + 8, :] = turned[4 * i:4 * i + 4, :]


    def read_lists():
        load_row.wait()
        load_col.wait()

        for k in range(LIST):
            pairs = row_v[:, k * 128:(k + 1) * 128] * BLK + col_v[:, k * 128:(k + 1) * 128]
            for s in range(STOPS):
                pair_v[s * LIST + k:s * LIST + k + 1, :] = pairs[s:s + 1, :]
        ask(0).start()
        ask(1).start()
        for n in range(FIRST, CHUNKS):
            send_main(n).start()
        prepare(0)
        load_slots(0).start()
        prepare(1)

    load_own.wait()

    lane_iota = lax.broadcasted_iota(jnp.int32, (8, 128), 1)
    sub_iota = lax.broadcasted_iota(jnp.int32, (8, 128), 0)
    tiles = (tile0, tile1)

    def multiply(step, n, on_core=None):
        tile = tiles[step % 2]
        if step == 0:
            lhs, rhs = buf[OWN], buf[OWN, rows_of(n)]
        elif step == 1:
            lhs, rhs = buf[OWN], buf[OTHER, rows_of(n)]
        elif step == 2 and on_core == 0:
            lhs, rhs = buf[OWN], buf[RIGHT, rows_of(n)]
        elif step == 2:
            lhs, rhs = buf[OTHER], buf[LEFT, rows_of(n)]
        elif step == 3:
            lhs, rhs = buf[LEFT], buf[RIGHT, rows_of(n)]
        else:
            lhs, rhs = own_quart[...], quart[rows_of(n)]
        product = lax.dot_general(lhs, rhs, (((1,), (1,)), ((), ())), preferred_element_type=jnp.float32)
        tile[pl.ds(pl.multiple_of(n * 2 * BLK, BLK), BLK), :] = product[:, :128]
        tile[pl.ds(pl.multiple_of(n * 2 * BLK + BLK, BLK), BLK), :] = product[:, 128:]

    def read_out(step, n, q):
        tile, here = tiles[step % 2], slots[step % 2]
        lanes = lane_v[pl.ds(pl.multiple_of(step * LIST * 2 + n * 8, 8), 8), :]
        found = jnp.zeros((8, 128), jnp.float32)
        for k in range(64):
            rows = None
            for s in range(8):
                at = here[q * ROWS + s % ROWS, s // ROWS * 64 + k]
                one = jnp.broadcast_to(tile[pl.ds(at, 1), :], (8, 128))
                rows = one if rows is None else jnp.where(sub_iota == s, one, rows)
            picked = jnp.take_along_axis(rows, lanes, axis=1)
            found = jnp.where(lane_iota == k, picked, found)
        turned = pltpu.roll(found, 64, 1)
        sums[step, pl.ds(n * ROWS, ROWS), :] = jnp.where(lane_iota[:ROWS] < 64, found[:ROWS], turned[ROWS:])

    def share(step, half):
        return sums.at[step, pl.ds(pl.multiple_of(half * SHARE, SHARE), SHARE)]

    def send_part(step, half, to, place, s):
        return pltpu.make_async_remote_copy(
            share(step, half), land.at[place, s], part_send.at[step, place % 2], part_recv.at[place, s],
            device_id=to, device_id_type=MESH)

    even_parts = {0: (0, 0, None, 0), 2: (1, 0, None, 0), 3: (2, 0, 1, 0), 4: (3, 1, 1, 2)}
    odd_parts = {0: (0, 0, None, 0), 1: (1, 0, None, 0), 2: (2, 1, 0, 0), 3: (3, 1, 0, 0), 4: (3, 0, None, 0)}

    def part_copies(step, parts):
        s, chip_step, to_core, place = parts[step]
        if to_core is None:
            return [send_part(step, 1 - snp, device(0, core, 1 - snp), 1, s)]
        return [send_part(step, snp, device(chip_step, to_core, snp), place, s),
                send_part(step, 1 - snp, device(chip_step, to_core, 1 - snp), place + 1, s)]

    def hand_out(step):
        for own, parts in ((even_core, even_parts), (odd_core, odd_parts)):
            if step in parts:
                @pl.when(own)
                def _():
                    for copy in part_copies(step, parts):
                        copy.start()
                    if parts[step][2] is None:
                        land[0, parts[step][0]] = share(step, snp)[...]

    for step in range(STEPS - 1):
        if step == 1:
            read_lists()
            send_sib.wait_recv()
        if step == 2:
            ask(0).wait_recv()
            ask(1).wait_recv()
            for later in range(2, STEPS):
                prepare(later)
        if step > 0:
            load_slots(step - 1).wait()
        if 0 < step < 3:
            load_slots(step).start()
        if step == 3:
            load_all_slots(3).start()

        @pl.loop(0, CHUNKS // UNROLL)
        def _(m):
            for q in range(UNROLL):
                n = m * UNROLL + q
                if step == 2:
                    send_main(n).wait_recv()

                    @pl.when(even_core)
                    def _():
                        pass_on(n).start()

                    if q == 0:
                        @pl.when(n == CHUNKS - UNROLL)
                        def _():
                            for i in range(CHUNKS):
                                send_main(i).wait_send()
                            for i in range(CHUNKS):
                                send_quarter(i).start()
                if step == 3:
                    @pl.when(odd_core)
                    def _():
                        pass_on(n).wait_recv()
                if step > 0:
                    @pl.when(m > 0)
                    def _():
                        reload_slots(step - 1, m - 1, q).wait()

                if step == 1:
                    @pl.when(odd_core)
                    def _():
                        multiply(step, n)
                        read_out(step - 1, n, q)

                    @pl.when(even_core)
                    def _():
                        read_out(step - 1, n, q)
                elif step == 2:
                    @pl.when(odd_core)
                    def _():
                        multiply(step, n)
                        read_out(step - 1, n, q)

                    @pl.when(even_core)
                    def _():
                        multiply(step, n, 0)
                elif step == 3:
                    @pl.when(core < 2)
                    def _():
                        multiply(step, n)
                        read_out(step - 1, n, q)
                else:
                    multiply(step, n)

                if step > 0:
                    @pl.when(m < CHUNKS // UNROLL - 1)
                    def _():
                        reload_slots(step - 1, m, q).start()
        if step > 0:
            hand_out(step - 1)

    load_all_slots(4).start()
    load_all_slots(3).wait()
    for n in range(CHUNKS):
        read_out(3, n, n)
    hand_out(3)
    load_part.wait()

    @pl.loop(0, CHUNKS // UNROLL)
    def _(m):
        for q in range(UNROLL):
            send_quarter(m * UNROLL + q).wait_recv()
            multiply(4, m * UNROLL + q)

    load_all_slots(4).wait()
    for n in range(CHUNKS):
        read_out(4, n, n)
    hand_out(4)

    for n in range(CHUNKS):
        send_quarter(n).wait_send()
    send_sib.wait_send()
    ask(0).wait_send()
    ask(1).wait_send()

    def landed(place, s):
        send_part(0, snp, sibling, place, s).wait_recv()

    for own, parts in ((even_core, even_parts), (odd_core, odd_parts)):
        @pl.when(own)
        def _():
            for step in parts:
                for copy in part_copies(step, parts):
                    copy.wait_send()
    for s in range(STOPS):
        landed(1, s)
    landed(0, 2)

    @pl.when(even_core)
    def _():
        for n in range(CHUNKS):
            pass_on(n).wait_send()
        landed(0, 3)

    @pl.when(odd_core)
    def _():
        landed(2, 3)
        landed(3, 3)
        land[0, 3] = land[0, 3] + (land[2, 3] + land[3, 3])

    for s in range(STOPS):
        both = land[0, s] + land[1, s]
        for k in range(SHARE):
            out[0, s:s + 1, k * 128:(k + 1) * 128] = both[k:k + 1, :]


def shards(dosage, pair_row, pair_col, pair_count):
    dma = pltpu.SemaphoreType.DMA
    sums = pl.pallas_call(
        kernel,
        out_shape=jax.ShapeDtypeStruct((1, STOPS, PAIRS // 2), jnp.float32),
        in_specs=[pl.BlockSpec(memory_space=pl.ANY)] * 3,
        out_specs=pl.BlockSpec(memory_space=pltpu.VMEM),
        scratch_shapes=[
            pltpu.VMEM((4, BLK, HALF), jnp.bfloat16),
            pltpu.VMEM((BLK, QUARTER), jnp.bfloat16),
            pltpu.VMEM((BLK, QUARTER), jnp.bfloat16),
            pltpu.VMEM((BLK * 16, 128), jnp.float32),
            pltpu.VMEM((BLK * 16, 128), jnp.float32),
            pltpu.VMEM((STOPS, PAIRS), jnp.int32),
            pltpu.VMEM((STOPS, PAIRS), jnp.int32),
            pltpu.VMEM((LISTS * LIST, 128), jnp.int32),
            pltpu.VMEM((STEPS * LIST, 128), jnp.int32),
            pltpu.VMEM((STEPS * LIST * 2, 128), jnp.int32),
            pltpu.SMEM((LIST, 128), jnp.int32),
            pltpu.SMEM((LIST, 128), jnp.int32),
            pltpu.VMEM((STEPS, LIST, 128), jnp.float32),
            pltpu.VMEM((4, STOPS, SHARE, 128), jnp.float32),
            dma, dma((3,)), dma((2, 1 + UNROLL)),
            dma((CHUNKS,)), dma((CHUNKS,)), dma((CHUNKS,)), dma((CHUNKS,)), dma((CHUNKS,)), dma((CHUNKS,)),
            dma, dma, dma((2,)), dma((2,)), dma((STEPS, 2)), dma((4, STOPS)),
        ],
        compiler_params=pltpu.CompilerParams(
            collective_id=0, has_side_effects=True, vmem_limit_bytes=56 << 20),
        cost_estimate=pl.CostEstimate(
            flops=2 * STOPS * BLK * BLK * HALF, bytes_accessed=2 * BLK * HALF * 2, transcendentals=0),
    )(dosage, pair_row, pair_col)
    slot = lax.axis_index("snp") * (PAIRS // 2) + jnp.arange(PAIRS // 2, dtype=jnp.int32)
    live = slot[None, None, :] < pair_count[:, :, None]
    return jnp.where(live, sums / SNPS, jnp.zeros_like(sums))


def solution(mesh):
    in_specs = (P("samp", "snp"), P("samp", None, None), P("samp", None, None), P("samp", None))
    out_specs = P("samp", None, "snp")
    return jax.shard_map(shards, mesh=mesh, in_specs=in_specs, out_specs=out_specs, check_vma=False)
```
